32 devices in a mesh: groups: 2 (over y), row: 4 (over z), col: 2 (over x), segment: 2 (over core).
Axes of the slice: x: 2, y: 2, z: 4, core: 2. Of those that a mesh axis runs over, the one named last changes fastest.
Arguments:
- latents: bfloat16 [4, 512, 3072], P(None, ('groups', 'col'), 'row'), parts along dimension 1, may hold values from -6 to 6
- w_in: bfloat16 [2, 3072, 12288], P('segment', 'col', 'row'), may hold values from -0.109375 to 0.109375
- b_in: float32 [2, 12288], P('segment', 'row'), may hold values from -4 to 4
- w_out: bfloat16 [2, 12288, 3072], P('segment', 'row', 'col'), may hold values from -0.0546875 to 0.0546875
- b_out: float32 [2, 3072], P('segment', 'row'), may hold values from -3 to 3
- modulation: float32 [2, 8, 3, 3072], P('segment', 'groups'), parts along dimension 1, may hold values from -3 to 3
Outputs:
- layer_outputs: bfloat16 [2, 4, 512, 3072], P('segment', None, ('groups', 'col'), 'row'), parts along dimension 2
The draws below stay inside these ranges and needn't reach their ends.
There are 2 independent parts, one for each index of `groups`. The reference program is written for one: setup_inputs(seed, part) draws one part's arguments, and reference() takes and returns one part's arrays. A program takes and returns all parts, laid end to end along the dimension named above; an argument that names none is the same for every part. Nothing has to cross between parts.
All inputs are finite; a program needn't handle non-finite values.
Results may differ from the reference program's by a relative error of at most 0.009.
Values may be sent and summed in bfloat16 or wider, within the bound.
A program may use at most 128 MiB of HBM per device.

```python
import jax
import jax.numpy as jnp
from jax import lax

D = 3072
FF = 12288
MB = 4
SEGMENTS = 2
TOKENS = 256
N_ROW = 4


def steps_of(own_key, shape, cuts, smallest, high):
    def one(position, blocks):
        draws = jax.random.uniform(jax.random.fold_in(jax.random.fold_in(own_key, 6), position), (blocks,), jnp.float32, smallest / len(cuts), high / len(cuts))
        return jnp.repeat(jnp.exp(draws), shape[position] // blocks).reshape((-1,) + (1,) * (len(shape) - position - 1))

    gain = one(*cuts[0])
    for cut in cuts[1:]:
        gain = gain * one(*cut)
    return gain


def normal_values(rng, shape, deviation, bound, shards=(), dtype=jnp.bfloat16):
    drawn = deviation * jax.random.normal(rng, shape, jnp.float32)
    if shards:
        drawn = drawn * steps_of(rng, shape, shards, -0.22, 0.18)
    return jnp.clip(drawn, -bound, bound).astype(dtype)


def setup_inputs(seed: int = 0, part: int = 0) -> dict:
    splits = jax.random.split(jax.random.key(seed), 7)
    part_splits = jax.random.split(jax.random.fold_in(splits[6], part), 7)
    return {
        "latents": normal_values(part_splits[0], (MB, TOKENS, D), 1.0, 6.0, ((1, 2), (2, 4))),
        "w_in": normal_values(splits[1], (SEGMENTS, D, FF), D ** -0.5, 0.109375, ((0, 2), (1, 2), (2, 4))),
        "b_in": normal_values(splits[2], (SEGMENTS, FF), 1.0, 4.0, ((0, 2), (1, 4)), jnp.float32),
        "w_out": normal_values(splits[3], (SEGMENTS, FF, D), FF ** -0.5, 0.0546875, ((0, 2), (1, 4), (2, 2))),
        "b_out": normal_values(splits[4], (SEGMENTS, D), 0.5, 3.0, ((0, 2), (1, 4)), jnp.float32),
        "modulation": normal_values(part_splits[5], (SEGMENTS, MB, 3, D), 0.5, 3.0, ((0, 2),), jnp.float32),
    }


def reference(latents, w_in, b_in, w_out, b_out, modulation):
    act = latents
    blocks = FF // N_ROW
    results = []
    for layer in range(SEGMENTS):
        values = act.astype(jnp.float32)
        mean = lax.optimization_barrier(jnp.mean(values, axis=-1, keepdims=True))
        var = lax.optimization_barrier(jnp.mean((values - mean) ** 2, axis=-1, keepdims=True))
        normed = (values - mean) * lax.rsqrt(var + 1e-06)
        shift = modulation[layer, :, 0][:, None, :]
        scale = modulation[layer, :, 1][:, None, :]
        gate = modulation[layer, :, 2][:, None, :]
        modulated = (normed * (1.0 + scale) + shift).astype(jnp.bfloat16)
        flat = modulated.reshape(MB * TOKENS, D)
        pre = jnp.dot(flat, w_in[layer], preferred_element_type=jnp.float32) + b_in[layer]
        hidden = jax.nn.gelu(pre, approximate=True).astype(jnp.bfloat16)
        branch = jnp.zeros((MB * TOKENS, D), jnp.float32)
        for block in range(N_ROW):
            part = jnp.dot(hidden[:, block * blocks:(block + 1) * blocks], w_out[layer, block * blocks:(block + 1) * blocks], preferred_element_type=jnp.float32)
            part = lax.optimization_barrier(part.astype(jnp.bfloat16))
            branch = branch + part.astype(jnp.float32)
        branch = branch.reshape(MB, TOKENS, D)
        act = (values + gate * (branch + b_out[layer])).astype(jnp.bfloat16)
        results.append(act)
    return jnp.stack(results)
```

```python
import functools

import jax
import jax.numpy as jnp
from jax import lax
from jax.experimental import pallas as pl
from jax.experimental.pallas import tpu as pltpu
from jax.sharding import PartitionSpec as P

MESH = pl.DeviceIdType.MESH
ROWS = 4
COLS = 2
SEGS = 2
BLOCK = 512


def shifted(block, axis, distance):
    devices = range(lax.axis_size(axis))
    route = [(i - distance, i) for i in devices if i - distance in devices]
    return lax.ppermute(block, axis, route)


def general(latents, w_in, b_in, w_out, b_out, modulation):
    panels = (
        lax.all_gather(w_in, "col", axis=1, tiled=True),
        lax.all_gather(w_out, "col", axis=2, tiled=True),
    )
    w_first = panels[0][0]
    w_second = panels[1][0]
    micro_count = latents.shape[0]
    width = latents.shape[2]
    segment = lax.axis_index("segment")
    segments = lax.axis_size("segment")
    ticks = micro_count + segments - 1
    row_start = lax.axis_index("row") * width
    conditioning = modulation[0]
    bias_first = b_in[0]
    bias_local = b_out[0]
    results = []
    handed = jnp.zeros_like(latents[0])
    for tick in range(ticks):
        if tick > 0:
            handed = shifted(results[-1], "segment", 1)
        first_feed = latents[min(tick, micro_count - 1)]
        feed = jnp.where(segment == 0, first_feed, handed)
        micro = jnp.clip(tick - segment, 0, micro_count - 1)
        mods = lax.dynamic_index_in_dim(conditioning, micro, 0, keepdims=False)
        values = feed.astype(jnp.float32)
        whole = lax.all_gather(feed, "row", axis=1, tiled=True).astype(jnp.float32)
        mean = jnp.mean(whole, axis=-1, keepdims=True)
        var = jnp.mean((whole - mean) ** 2, axis=-1, keepdims=True)
        normed = (whole - mean) * lax.rsqrt(var + 1e-06)
        modulated = (normed * (1.0 + mods[1]) + mods[0]).astype(jnp.bfloat16)
        pre = jnp.dot(modulated, w_first, preferred_element_type=jnp.float32)
        hidden = jax.nn.gelu(pre + bias_first, approximate=True).astype(jnp.bfloat16)
        term = jnp.dot(hidden, w_second, preferred_element_type=jnp.float32)
        branch = lax.psum_scatter(
            term.astype(jnp.bfloat16), "row", scatter_dimension=1, tiled=True
        ).astype(jnp.float32)
        gate_local = lax.dynamic_slice_in_dim(mods[2], row_start, width, 0)
        results.append((values + gate_local * (branch + bias_local)).astype(jnp.bfloat16))
    stacked = jnp.stack(results)
    chosen = lax.dynamic_slice_in_dim(stacked, segment, micro_count, 0)
    return chosen[None]


def gelu(v):
    return 0.5 * v * (1.0 + jnp.tanh(0.7978845608 * (v + 0.044715 * (v * v * v))))


def kernel(
    micros, blocks, own_ref, win_hbm, bin_ref, wout_hbm, bout_ref, shift_ref, scale_ref, gate_ref,
    out_ref,
    win, wout, feed, ready, pre, xsend, xrecv, total, psend, precv, ssend, srecv,
    wsem, xs_sem, xr_sem, ss_sem, sr_sem, ps_sem, pr_sem, as_sem, ar_sem,
):
    row = lax.axis_index("row")
    col = lax.axis_index("col")
    seg = lax.axis_index("segment")
    other_col = 1 - col
    part = own_ref.shape[2]
    half = part * ROWS

    load_in = pltpu.make_async_copy(win_hbm, win, wsem.at[0])
    load_out = pltpu.make_async_copy(wout_hbm, wout, wsem.at[1])
    load_in.start()
    load_out.start()

    def row_at(k):
        return lax.rem(row + k, ROWS)

    barrier = pltpu.get_barrier_semaphore()
    pl.semaphore_signal(barrier, inc=1, device_id={"col": other_col}, device_id_type=MESH)
    for k in range(1, ROWS):
        pl.semaphore_signal(barrier, inc=1, device_id={"row": row_at(k)}, device_id_type=MESH)
    for k in range(ROWS):
        pl.semaphore_signal(
            barrier, inc=1, device_id={"row": row_at(k), "segment": 1 - seg}, device_id_type=MESH
        )
    pl.semaphore_wait(barrier, 2 * ROWS)

    def exchange(m, j):
        return pltpu.make_async_remote_copy(
            src_ref=xsend.at[m, j], dst_ref=xrecv.at[m, j],
            send_sem=xs_sem.at[m, j], recv_sem=xr_sem.at[m, j],
            device_id={"col": other_col}, device_id_type=MESH,
        )

    def moments(m):
        return pltpu.make_async_remote_copy(
            src_ref=ssend.at[m], dst_ref=srecv.at[m],
            send_sem=ss_sem.at[m], recv_sem=sr_sem.at[m],
            device_id={"col": other_col}, device_id_type=MESH,
        )

    def partial(m, k):
        return pltpu.make_async_remote_copy(
            src_ref=psend.at[m, row_at(k)], dst_ref=precv.at[m, k],
            send_sem=ps_sem.at[m, k], recv_sem=pr_sem.at[m, k],
            device_id={"row": row_at(k)}, device_id_type=MESH,
        )

    def first_feed(m, k):
        return pltpu.make_async_remote_copy(
            src_ref=own_ref.at[m], dst_ref=feed.at[m, row],
            send_sem=as_sem.at[m, k], recv_sem=ar_sem.at[m, k],
            device_id={"row": row_at(k)}, device_id_type=MESH,
        )

    def next_feed(m, k):
        return pltpu.make_async_remote_copy(
            src_ref=out_ref.at[m], dst_ref=feed.at[m, row],
            send_sem=as_sem.at[m, k], recv_sem=ar_sem.at[m, k],
            device_id={"row": row_at(k), "segment": 1}, device_id_type=MESH,
        )

    def measure(m):
        sums = jnp.zeros((feed.shape[2], 1), jnp.float32)
        for q in range(ROWS):
            sums += jnp.sum(feed[m, q].astype(jnp.float32), axis=-1, keepdims=True)
        mean = sums / half
        spread = jnp.zeros_like(sums)
        for q in range(ROWS):
            off = feed[m, q].astype(jnp.float32) - mean
            spread += jnp.sum(off * off, axis=-1, keepdims=True)
        lane = lax.broadcasted_iota(jnp.int32, ssend.shape[1:], 1)
        ssend[m] = jnp.where(lane == 0, mean, spread)
        moments(m).start()

    def enter(m):
        @pl.when(seg == 1)
        def _():
            for k in range(ROWS):
                next_feed(m, k).wait_recv()
            measure(m)

        moments(m).wait_recv()
        mine, theirs = ssend[m], srecv[m]
        gap = mine[:, 0:1] - theirs[:, 0:1]
        mean = 0.5 * (mine[:, 0:1] + theirs[:, 0:1])
        var = (mine[:, 1:2] + theirs[:, 1:2] + (0.5 * half) * gap * gap) / (2 * half)
        inverse = lax.rsqrt(var + 1e-06)
        for q in range(ROWS):
            at = pl.ds(q * part, part)
            normed = (feed[m, q].astype(jnp.float32) - mean) * inverse
            ready[:, at] = (
                normed * (1.0 + scale_ref[m, :, at]) + shift_ref[m, :, at]
            ).astype(jnp.bfloat16)

        @pl.loop(0, blocks)
        def _(j):
            at = pl.ds(pl.multiple_of(j * BLOCK, BLOCK), BLOCK)
            product = jnp.dot(ready[...], win[:, at], preferred_element_type=jnp.float32)
            xsend[m, j] = product.astype(jnp.bfloat16)
            exchange(m, j).start()
            pre[lax.rem(m, 2), j] = product + bin_ref[:, at]

    def middle(m):
        total[...] = jnp.zeros_like(total)

        @pl.loop(0, blocks)
        def _(j):
            exchange(m, j).wait_recv()
            at = pl.ds(pl.multiple_of(j * BLOCK, BLOCK), BLOCK)
            hidden = gelu(pre[lax.rem(m, 2), j] + xrecv[m, j].astype(jnp.float32))
            total[...] += jnp.dot(
                hidden.astype(jnp.bfloat16), wout[at, :], preferred_element_type=jnp.float32
            )

        for q in range(ROWS):
            psend[m, q] = total[:, q * part:(q + 1) * part].astype(jnp.bfloat16)
        for k in range(1, ROWS):
            partial(m, k).start()

    def leave(m):
        branch = psend[m, row].astype(jnp.float32)
        for k in range(1, ROWS):
            partial(m, k).wait_recv()
            branch += precv[m, k].astype(jnp.float32)
        act = feed[m, row].astype(jnp.float32) + gate_ref[m] * (branch + bout_ref[...])
        out_ref[m] = act.astype(jnp.bfloat16)

        @pl.when(seg == 0)
        def _():
            for k in range(ROWS):
                next_feed(m, k).start()

    @pl.when(seg == 0)
    def _():
        @pl.loop(0, micros)
        def _(m):
            for k in range(1, ROWS):
                first_feed(m, k).start()
            feed[m, row] = own_ref[m]

        @pl.loop(0, micros)
        def _(m):
            for k in range(1, ROWS):
                first_feed(m, k).wait_recv()
            measure(m)

        @pl.loop(0, micros)
        def _(m):
            for k in range(1, ROWS):
                first_feed(m, k).wait_send()

    load_in.wait()
    load_out.wait()

    @pl.loop(0, micros + 2)
    def _(i):
        @pl.when(i >= 2)
        def _():
            leave(i - 2)

        @pl.when(i < micros)
        def _():
            enter(i)

        @pl.when((i >= 1) & (i <= micros))
        def _():
            middle(i - 1)

    @pl.loop(0, micros)
    def _(m):
        moments(m).wait_send()
        for k in range(1, ROWS):
            partial(m, k).wait_send()

        @pl.loop(0, blocks)
        def _(j):
            exchange(m, j).wait_send()

        @pl.when(seg == 0)
        def _():
            for k in range(ROWS):
                next_feed(m, k).wait_send()


def layers(own, w_first, bias_first, w_second, bias_last, shift, scale, gate):
    micros, tokens, part = own.shape
    half, units = w_first.shape
    blocks = units // BLOCK
    vmem = pl.BlockSpec(memory_space=pltpu.VMEM)
    hbm = pl.BlockSpec(memory_space=pl.ANY)
    bf16, f32, dma = jnp.bfloat16, jnp.float32, pltpu.SemaphoreType.DMA
    return pl.pallas_call(
        functools.partial(kernel, micros, blocks),
        out_shape=jax.ShapeDtypeStruct(own.shape, bf16),
        in_specs=[vmem, hbm, vmem, hbm, vmem, vmem, vmem, vmem],
        out_specs=vmem,
        scratch_shapes=[
            pltpu.VMEM((half, units), bf16),
            pltpu.VMEM((units, half), bf16),
            pltpu.VMEM((micros, ROWS, tokens, part), bf16),
            pltpu.VMEM((tokens, half), bf16),
            pltpu.VMEM((2, blocks, tokens, BLOCK), f32),
            pltpu.VMEM((micros, blocks, tokens, BLOCK), bf16),
            pltpu.VMEM((micros, blocks, tokens, BLOCK), bf16),
            pltpu.VMEM((tokens, half), f32),
            pltpu.VMEM((micros, ROWS, tokens, part), bf16),
            pltpu.VMEM((micros, ROWS, tokens, part), bf16),
            pltpu.VMEM((micros, tokens, 128), f32),
            pltpu.VMEM((micros, tokens, 128), f32),
            dma((2,)),
            dma((micros, blocks)),
            dma((micros, blocks)),
            dma((micros,)),
            dma((micros,)),
            dma((micros, ROWS)),
            dma((micros, ROWS)),
            dma((micros, ROWS)),
            dma((micros, ROWS)),
        ],
        compiler_params=pltpu.CompilerParams(
            collective_id=0, has_side_effects=True, vmem_limit_bytes=62 * 1024 * 1024
        ),
        cost_estimate=pl.CostEstimate(
            flops=4 * micros * tokens * half * units,
            bytes_accessed=4 * half * units,
            transcendentals=micros * tokens * units,
        ),
    )(own, w_first, bias_first, w_second, bias_last, shift, scale, gate)


def stationary(latents, w_in, b_in, w_out, b_out, modulation):
    row, col = lax.axis_index("row"), lax.axis_index("col")
    width = latents.shape[2]
    part = width // 2
    here = latents.shape[1]
    half = w_in.shape[1]

    def place(r, c):
        return r * COLS + c

    def route(k):
        return [
            (place(r, c), place(2 * (r % 2) + (c + k) % 2, r // 2))
            for r in range(ROWS) for c in range(COLS)
        ]

    parts = []
    for k in range(2):
        piece = lax.dynamic_slice_in_dim(latents, lax.rem(col + k, 2) * part, part, 2)
        parts.append(lax.ppermute(piece, ("row", "col"), route(k)))
    even = lax.rem(row, 2) == 0
    own = jnp.concatenate(
        [jnp.where(even, parts[0], parts[1]), jnp.where(even, parts[1], parts[0])], axis=1
    )
    bias_last = lax.ppermute(
        lax.dynamic_slice_in_dim(b_out, col * part, part, 1), ("row", "col"), route(0)
    )
    mods = modulation[0]
    shift = lax.dynamic_slice_in_dim(mods[:, 0:1], col * half, half, 2)
    scale = lax.dynamic_slice_in_dim(mods[:, 1:2], col * half, half, 2)
    gate = lax.dynamic_slice_in_dim(mods[:, 2:3], col * half + row * part, part, 2)
    done = layers(own, w_in[0], b_in, w_out[0], bias_last, shift, scale, gate)
    parts = []
    for k in range(2):
        piece = lax.dynamic_slice_in_dim(done, lax.rem(row + k, 2) * here, here, 1)
        back = [(b, a) for a, b in route(k)]
        parts.append(lax.ppermute(piece, ("row", "col"), back))
    first = col == 0
    return jnp.concatenate(
        [jnp.where(first, parts[0], parts[1]), jnp.where(first, parts[1], parts[0])], axis=2
    )[None]


def solution(mesh):
    sizes = dict(mesh.shape)
    fits = (sizes["row"], sizes["col"], sizes["segment"]) == (ROWS, COLS, SEGS)

    def on_device(latents, w_in, *rest):
        aligned = latents.shape[2] % 256 == 0 and w_in.shape[2] % BLOCK == 0
        chosen = stationary if fits and aligned else general
        return chosen(latents, w_in, *rest)

    return jax.shard_map(
        on_device,
        mesh=mesh,
        in_specs=(
            P(None, ("groups", "col"), "row"),
            P("segment", "col", "row"),
            P("segment", "row"),
            P("segment", "row", "col"),
            P("segment", "row"),
            P("segment", "groups", None, None),
        ),
        out_specs=P("segment", None, ("groups", "col"), "row"),
        check_vma=False,
    )
```

```python
import functools

import jax
import jax.numpy as jnp
from jax import lax
from jax.experimental import pallas as pl
from jax.experimental.pallas import tpu as pltpu
from jax.sharding import PartitionSpec as P

MESH = pl.DeviceIdType.MESH
ROWS = 4
COLS = 2
SEGS = 2
BLOCK = 512


def shifted(block, axis, distance):
    devices = range(lax.axis_size(axis))
    route = [(i - distance, i) for i in devices if i - distance in devices]
    return lax.ppermute(block, axis, route)


def general(latents, w_in, b_in, w_out, b_out, modulation):
    panels = (
        lax.all_gather(w_in, "col", axis=1, tiled=True),
        lax.all_gather(w_out, "col", axis=2, tiled=True),
    )
    w_first = panels[0][0]
    w_second = panels[1][0]
    micro_count = latents.shape[0]
    width = latents.shape[2]
    segment = lax.axis_index("segment")
    segments = lax.axis_size("segment")
    ticks = micro_count + segments - 1
    row_start = lax.axis_index("row") * width
    conditioning = modulation[0]
    bias_first = b_in[0]
    bias_local = b_out[0]
    results = []
    handed = jnp.zeros_like(latents[0])
    for tick in range(ticks):
        if tick > 0:
            handed = shifted(results[-1], "segment", 1)
        first_feed = latents[min(tick, micro_count - 1)]
        feed = jnp.where(segment == 0, first_feed, handed)
        micro = jnp.clip(tick - segment, 0, micro_count - 1)
        mods = lax.dynamic_index_in_dim(conditioning, micro, 0, keepdims=False)
        values = feed.astype(jnp.float32)
        whole = lax.all_gather(feed, "row", axis=1, tiled=True).astype(jnp.float32)
        mean = jnp.mean(whole, axis=-1, keepdims=True)
        var = jnp.mean((whole - mean) ** 2, axis=-1, keepdims=True)
        normed = (whole - mean) * lax.rsqrt(var + 1e-06)
        modulated = (normed * (1.0 + mods[1]) + mods[0]).astype(jnp.bfloat16)
        pre = jnp.dot(modulated, w_first, preferred_element_type=jnp.float32)
        hidden = jax.nn.gelu(pre + bias_first, approximate=True).astype(jnp.bfloat16)
        term = jnp.dot(hidden, w_second, preferred_element_type=jnp.float32)
        branch = lax.psum_scatter(
            term.astype(jnp.bfloat16), "row", scatter_dimension=1, tiled=True
        ).astype(jnp.float32)
        gate_local = lax.dynamic_slice_in_dim(mods[2], row_start, width, 0)
        results.append((values + gate_local * (branch + bias_local)).astype(jnp.bfloat16))
    stacked = jnp.stack(results)
    chosen = lax.dynamic_slice_in_dim(stacked, segment, micro_count, 0)
    return chosen[None]


def gelu(v):
    return 0.5 * v * (1.0 + jnp.tanh(0.7978845608 * (v + 0.044715 * (v * v * v))))


def kernel(
    micros, blocks, lat_ref, win_hbm, bin_ref, wout_hbm, bout_ref, mods_ref,
    out_ref,
    win, wout, feed, ready, pre, xsend, xrecv, total, psend, precv, ssend, srecv, result, landed, bout,
    wsem, xs_sem, xr_sem, ss_sem, sr_sem, ps_sem, pr_sem, as_sem, ar_sem,
    is_sem, ir_sem, os_sem, or_sem, bs_sem, br_sem,
):
    row = lax.axis_index("row")
    col = lax.axis_index("col")
    seg = lax.axis_index("segment")
    here, width = lat_ref.shape[1:]
    part = width // 2
    half = part * ROWS

    load_in = pltpu.make_async_copy(win_hbm, win, wsem.at[0])
    load_out = pltpu.make_async_copy(wout_hbm, wout, wsem.at[1])
    load_in.start()
    load_out.start()

    def row_at(k):
        return lax.rem(row + k, ROWS)

    placed_row = 2 * col + row // 2
    work_col = row // 2

    def work_row(h):
        return 2 * lax.rem(row, 2) + h

    def works_own(h):
        return (work_row(h) == row) & (work_col == col)

    barrier = pltpu.get_barrier_semaphore()
    for k in range(ROWS):
        for c in range(COLS):
            for g in range(SEGS):
                if k or c or g:
                    pl.semaphore_signal(
                        barrier, inc=1, device_id_type=MESH,
                        device_id={
                            "row": row_at(k), "col": lax.rem(col + c, COLS), "segment": lax.rem(seg + g, SEGS)
                        },
                    )
    pl.semaphore_wait(barrier, ROWS * COLS * SEGS - 1)

    def exchange(m, j):
        return pltpu.make_async_remote_copy(
            src_ref=xsend.at[m, j], dst_ref=xrecv.at[m, j],
            send_sem=xs_sem.at[m, j], recv_sem=xr_sem.at[m, j],
            device_id={"col": 1 - col}, device_id_type=MESH,
        )

    def moments(m):
        return pltpu.make_async_remote_copy(
            src_ref=ssend.at[m], dst_ref=srecv.at[m],
            send_sem=ss_sem.at[m], recv_sem=sr_sem.at[m],
            device_id={"col": 1 - col}, device_id_type=MESH,
        )

    def partial(m, k):
        return pltpu.make_async_remote_copy(
            src_ref=psend.at[m, row_at(k)], dst_ref=precv.at[m, k],
            send_sem=ps_sem.at[m, k], recv_sem=pr_sem.at[m, k],
            device_id={"row": row_at(k)}, device_id_type=MESH,
        )

    def first_feed(m, k):
        return pltpu.make_async_remote_copy(
            src_ref=feed.at[m, row], dst_ref=feed.at[m, row],
            send_sem=as_sem.at[m, k], recv_sem=ar_sem.at[m, k],
            device_id={"row": row_at(k)}, device_id_type=MESH,
        )

    def next_feed(m, k):
        return pltpu.make_async_remote_copy(
            src_ref=result.at[m], dst_ref=feed.at[m, row],
            send_sem=as_sem.at[m, k], recv_sem=ar_sem.at[m, k],
            device_id={"row": row_at(k), "segment": 1}, device_id_type=MESH,
        )

    def mine_at(c):
        return pl.ds(pl.multiple_of(c * here, here), here)

    def latent(m, h, c):
        return pltpu.make_async_remote_copy(
            src_ref=lat_ref.at[m, :, pl.ds(h * part, part)],
            dst_ref=feed.at[m, work_row(h), mine_at(col)],
            send_sem=is_sem.at[m, h], recv_sem=ir_sem.at[m, c],
            device_id={"row": work_row(h), "col": work_col}, device_id_type=MESH,
        )

    def finished(m, c, h):
        at = pl.ds(pl.multiple_of(lax.rem(row, 2) * part, 128), part)
        return pltpu.make_async_remote_copy(
            src_ref=result.at[m, pl.ds(c * here, here)],
            dst_ref=landed.at[m, :, at],
            send_sem=os_sem.at[m, c], recv_sem=or_sem.at[m, h],
            device_id={"row": placed_row, "col": c}, device_id_type=MESH,
        )

    def last_bias():
        return pltpu.make_async_remote_copy(
            src_ref=bout_ref.at[:, pl.ds(pl.multiple_of(col * part, 128), part)], dst_ref=bout,
            send_sem=bs_sem.at[0], recv_sem=br_sem.at[0],
            device_id={"row": work_row(col), "col": work_col}, device_id_type=MESH,
        )

    def send_latents(m):
        for h in range(2):
            own = works_own(h)

            @pl.when(own)
            def _():
                feed[m, row, mine_at(col)] = lat_ref[m, :, h * part:(h + 1) * part]

            @pl.when(jnp.logical_not(own))
            def _():
                latent(m, h, col).start()

    def spread_latents(m):
        for c in range(COLS):
            @pl.when(jnp.logical_not((placed_row == row) & (col == c)))
            def _():
                latent(m, 0, c).wait_recv()
        for k in range(1, ROWS):
            first_feed(m, k).start()

    def measure(m):
        @pl.when(seg == 0)
        def _():
            for k in range(1, ROWS):
                first_feed(m, k).wait_recv()

        @pl.when(seg == 1)
        def _():
            for k in range(ROWS):
                next_feed(m, k).wait_recv()

        sums = jnp.zeros((feed.shape[2], 1), jnp.float32)
        for q in range(ROWS):
            sums += jnp.sum(feed[m, q].astype(jnp.float32), axis=-1, keepdims=True)
        mean = sums / half
        spread = jnp.zeros_like(sums)
        for q in range(ROWS):
            off = feed[m, q].astype(jnp.float32) - mean
            spread += jnp.sum(off * off, axis=-1, keepdims=True)
        lane = lax.broadcasted_iota(jnp.int32, ssend.shape[1:], 1)
        ssend[m] = jnp.where(lane == 0, mean, spread)
        moments(m).start()

    def enter(m):
        moments(m).wait_recv()
        mine, theirs = ssend[m], srecv[m]
        gap = mine[:, 0:1] - theirs[:, 0:1]
        mean = 0.5 * (mine[:, 0:1] + theirs[:, 0:1])
        var = (mine[:, 1:2] + theirs[:, 1:2] + (0.5 * half) * gap * gap) / (2 * half)
        inverse = lax.rsqrt(var + 1e-06)
        for q in range(ROWS):
            at = pl.ds(pl.multiple_of(col * half + q * part, 128), part)
            normed = (feed[m, q].astype(jnp.float32) - mean) * inverse
            ready[:, q * part:(q + 1) * part] = (
                normed * (1.0 + mods_ref[m, 1:2, at]) + mods_ref[m, 0:1, at]
            ).astype(jnp.bfloat16)

        @pl.when((m + 1 < micros) & ((seg == 1) | (m >= 1)))
        def _():
            measure(m + 1)

        @pl.loop(0, blocks)
        def _(j):
            at = pl.ds(pl.multiple_of(j * BLOCK, BLOCK), BLOCK)
            product = jnp.dot(ready[...], win[:, at], preferred_element_type=jnp.float32)
            xsend[m, j] = product.astype(jnp.bfloat16)
            exchange(m, j).start()
            pre[lax.rem(m, 2), j] = product + bin_ref[:, at]

        @pl.when(seg == 0)
        def _():
            @pl.when((m == 0) & (micros > 1))
            def _():
                measure(m + 1)

            @pl.when(m + 2 < micros)
            def _():
                spread_latents(m + 2)

    def middle(m):
        total[...] = jnp.zeros_like(total)

        @pl.loop(0, blocks)
        def _(j):
            exchange(m, j).wait_recv()
            at = pl.ds(pl.multiple_of(j * BLOCK, BLOCK), BLOCK)
            hidden = gelu(pre[lax.rem(m, 2), j] + xrecv[m, j].astype(jnp.float32))
            total[...] += jnp.dot(
                hidden.astype(jnp.bfloat16), wout[at, :], preferred_element_type=jnp.float32
            )

        for q in range(ROWS):
            psend[m, q] = total[:, q * part:(q + 1) * part].astype(jnp.bfloat16)
        for k in range(1, ROWS):
            partial(m, k).start()

    def leave(m):
        branch = psend[m, row].astype(jnp.float32)
        for k in range(1, ROWS):
            partial(m, k).wait_recv()
            branch += precv[m, k].astype(jnp.float32)
        at = pl.ds(pl.multiple_of(col * half + row * part, 128), part)
        act = feed[m, row].astype(jnp.float32) + mods_ref[m, 2:3, at] * (branch + bout[0:1, :])
        result[m] = act.astype(jnp.bfloat16)

        @pl.when(seg == 0)
        def _():
            for k in range(ROWS):
                next_feed(m, k).start()

        for c in range(COLS):
            own = (placed_row == row) & (col == c)

            @pl.when(jnp.logical_not(own))
            def _():
                finished(m, c, lax.rem(row, 2)).start()

            for h in range(2):
                @pl.when(own & (lax.rem(row, 2) == h))
                def _():
                    landed[m, :, h * part:(h + 1) * part] = result[m, c * here:(c + 1) * here]

    @pl.when(seg == 0)
    def _():
        @pl.loop(0, micros)
        def _(m):
            send_latents(m)

    own_bias = works_own(col)

    @pl.when(own_bias)
    def _():
        for h in range(2):
            @pl.when(col == h)
            def _():
                bout[...] = bout_ref[:, h * part:(h + 1) * part]

    @pl.when(jnp.logical_not(own_bias))
    def _():
        last_bias().start()

    @pl.when(seg == 0)
    def _():
        spread_latents(0)
        if micros > 1:
            spread_latents(1)

    measure(0)
    load_in.wait()

    @pl.loop(0, micros + 2)
    def _(i):
        @pl.when(i < micros)
        def _():
            enter(i)

        @pl.when(i == 1)
        def _():
            load_out.wait()

            @pl.when(jnp.logical_not((placed_row == row) & (lax.rem(row, 2) == col)))
            def _():
                last_bias().wait_recv()

        @pl.when(i >= 2)
        def _():
            leave(i - 2)

        @pl.when((i >= 1) & (i <= micros))
        def _():
            middle(i - 1)

    @pl.when(jnp.logical_not(own_bias))
    def _():
        last_bias().wait_send()

    @pl.loop(0, micros)
    def _(m):
        for h in range(2):
            @pl.when(jnp.logical_not(works_own(h)))
            def _():
                finished(m, 0, h).wait_recv()

        out_ref[m] = landed[m]
        moments(m).wait_send()
        for k in range(1, ROWS):
            partial(m, k).wait_send()

        @pl.loop(0, blocks)
        def _(j):
            exchange(m, j).wait_send()

        for c in range(COLS):
            @pl.when(jnp.logical_not((placed_row == row) & (col == c)))
            def _():
                finished(m, c, 0).wait_send()

        @pl.when(seg == 0)
        def _():
            for k in range(ROWS):
                next_feed(m, k).wait_send()
            for k in range(1, ROWS):
                first_feed(m, k).wait_send()
            for h in range(2):
                @pl.when(jnp.logical_not(works_own(h)))
                def _():
                    latent(m, h, 0).wait_send()


def stationary(latents, w_in, b_in, w_out, b_out, modulation):
    micros, here, width = latents.shape
    tokens, part = COLS * here, width // 2
    half, units = w_in.shape[1:]
    blocks = units // BLOCK
    vmem = pl.BlockSpec(memory_space=pltpu.VMEM)
    hbm = pl.BlockSpec(memory_space=pl.ANY)
    bf16, f32, dma = jnp.bfloat16, jnp.float32, pltpu.SemaphoreType.DMA
    done = pl.pallas_call(
        functools.partial(kernel, micros, blocks),
        out_shape=jax.ShapeDtypeStruct(latents.shape, bf16),
        in_specs=[vmem, hbm, vmem, hbm, vmem, vmem],
        out_specs=vmem,
        scratch_shapes=[
            pltpu.VMEM((half, units), bf16),
            pltpu.VMEM((units, half), bf16),
            pltpu.VMEM((micros, ROWS, tokens, part), bf16),
            pltpu.VMEM((tokens, half), bf16),
            pltpu.VMEM((2, blocks, tokens, BLOCK), f32),
            pltpu.VMEM((micros, blocks, tokens, BLOCK), bf16),
            pltpu.VMEM((micros, blocks, tokens, BLOCK), bf16),
            pltpu.VMEM((tokens, half), f32),
            pltpu.VMEM((micros, ROWS, tokens, part), bf16),
            pltpu.VMEM((micros, ROWS, tokens, part), bf16),
            pltpu.VMEM((micros, tokens, 128), f32),
            pltpu.VMEM((micros, tokens, 128), f32),
            pltpu.VMEM((micros, tokens, part), bf16),
            pltpu.VMEM((micros, here, width), bf16),
            pltpu.VMEM((8, part), f32),
            dma((2,)),
            dma((micros, blocks)),
            dma((micros, blocks)),
            dma((micros,)),
            dma((micros,)),
            dma((micros, ROWS)),
            dma((micros, ROWS)),
            dma((micros, ROWS)),
            dma((micros, ROWS)),
            dma((micros, 2)),
            dma((micros, COLS)),
            dma((micros, COLS)),
            dma((micros, 2)),
            dma((1,)),
            dma((1,)),
        ],
        compiler_params=pltpu.CompilerParams(
            collective_id=0, has_side_effects=True, vmem_limit_bytes=62 * 1024 * 1024
        ),
        cost_estimate=pl.CostEstimate(
            flops=4 * micros * tokens * half * units,
            bytes_accessed=4 * half * units,
            transcendentals=micros * tokens * units,
        ),
    )(latents, w_in[0], b_in, w_out[0], jnp.broadcast_to(b_out, (8, width)), modulation[0])
    return done[None]


def solution(mesh):
    sizes = dict(mesh.shape)
    fits = (sizes["row"], sizes["col"], sizes["segment"]) == (ROWS, COLS, SEGS)

    def on_device(latents, w_in, *rest):
        aligned = latents.shape[2] % 256 == 0 and w_in.shape[2] % BLOCK == 0
        chosen = stationary if fits and aligned else general
        return chosen(latents, w_in, *rest)

    return jax.shard_map(
        on_device,
        mesh=mesh,
        in_specs=(
            P(None, ("groups", "col"), "row"),
            P("segment", "col", "row"),
            P("segment", "row"),
            P("segment", "row", "col"),
            P("segment", "row"),
            P("segment", "groups", None, None),
        ),
        out_specs=P("segment", None, ("groups", "col"), "row"),
        check_vma=False,
    )
```

```python
import functools

import jax
import jax.numpy as jnp
from jax import lax
from jax.experimental import pallas as pl
from jax.experimental.pallas import tpu as pltpu
from jax.sharding import PartitionSpec as P

MESH = pl.DeviceIdType.MESH
ROWS = 4
COLS = 2
SEGS = 2
BLOCK = 512


def shifted(block, axis, distance):
    devices = range(lax.axis_size(axis))
    route = [(i - distance, i) for i in devices if i - distance in devices]
    return lax.ppermute(block, axis, route)


def general(latents, w_in, b_in, w_out, b_out, modulation):
    panels = (
        lax.all_gather(w_in, "col", axis=1, tiled=True),
        lax.all_gather(w_out, "col", axis=2, tiled=True),
    )
    w_first = panels[0][0]
    w_second = panels[1][0]
    micro_count = latents.shape[0]
    width = latents.shape[2]
    segment = lax.axis_index("segment")
    segments = lax.axis_size("segment")
    ticks = micro_count + segments - 1
    row_start = lax.axis_index("row") * width
    conditioning = modulation[0]
    bias_first = b_in[0]
    bias_local = b_out[0]
    results = []
    handed = jnp.zeros_like(latents[0])
    for tick in range(ticks):
        if tick > 0:
            handed = shifted(results[-1], "segment", 1)
        first_feed = latents[min(tick, micro_count - 1)]
        feed = jnp.where(segment == 0, first_feed, handed)
        micro = jnp.clip(tick - segment, 0, micro_count - 1)
        mods = lax.dynamic_index_in_dim(conditioning, micro, 0, keepdims=False)
        values = feed.astype(jnp.float32)
        whole = lax.all_gather(feed, "row", axis=1, tiled=True).astype(jnp.float32)
        mean = jnp.mean(whole, axis=-1, keepdims=True)
        var = jnp.mean((whole - mean) ** 2, axis=-1, keepdims=True)
        normed = (whole - mean) * lax.rsqrt(var + 1e-06)
        modulated = (normed * (1.0 + mods[1]) + mods[0]).astype(jnp.bfloat16)
        pre = jnp.dot(modulated, w_first, preferred_element_type=jnp.float32)
        hidden = jax.nn.gelu(pre + bias_first, approximate=True).astype(jnp.bfloat16)
        term = jnp.dot(hidden, w_second, preferred_element_type=jnp.float32)
        branch = lax.psum_scatter(
            term.astype(jnp.bfloat16), "row", scatter_dimension=1, tiled=True
        ).astype(jnp.float32)
        gate_local = lax.dynamic_slice_in_dim(mods[2], row_start, width, 0)
        results.append((values + gate_local * (branch + bias_local)).astype(jnp.bfloat16))
    stacked = jnp.stack(results)
    chosen = lax.dynamic_slice_in_dim(stacked, segment, micro_count, 0)
    return chosen[None]


def gelu(v):
    return 0.5 * v * (1.0 + jnp.tanh(0.7978845608 * (v + 0.044715 * (v * v * v))))


def kernel(
    micros, blocks, lat_ref, win_hbm, bin_ref, wout_hbm, bout_ref, mods_ref,
    out_ref,
    win, wout, feed, ready, pre, xsend, xrecv, total, psend, precv, ssend, srecv, result, landed, bout,
    wsem, xs_sem, xr_sem, ss_sem, sr_sem, ps_sem, pr_sem, as_sem, ar_sem,
    is_sem, ir_sem, os_sem, or_sem, bs_sem, br_sem, fs_sem, ns_sem,
):
    row = lax.axis_index("row")
    col = lax.axis_index("col")
    seg = lax.axis_index("segment")
    here, width = lat_ref.shape[1:]
    part = width // 2
    half = part * ROWS

    load_in = pltpu.make_async_copy(win_hbm, win, wsem.at[0])
    load_out = pltpu.make_async_copy(wout_hbm, wout, wsem.at[1])
    load_in.start()
    load_out.start()

    def row_at(k):
        return lax.rem(row + k, ROWS)

    placed_row = 2 * col + row // 2
    work_col = row // 2

    def work_row(h):
        return 2 * lax.rem(row, 2) + h

    def works_own(h):
        return (work_row(h) == row) & (work_col == col)

    barrier = pltpu.get_barrier_semaphore()
    for k in range(ROWS):
        for c in range(COLS):
            for g in range(SEGS):
                if k or c or g:
                    pl.semaphore_signal(
                        barrier, inc=1, device_id_type=MESH,
                        device_id={
                            "row": row_at(k), "col": lax.rem(col + c, COLS), "segment": lax.rem(seg + g, SEGS)
                        },
                    )
    pl.semaphore_wait(barrier, ROWS * COLS * SEGS - 1)

    def exchange(m, j):
        return pltpu.make_async_remote_copy(
            src_ref=xsend.at[m, j], dst_ref=xrecv.at[m, j],
            send_sem=xs_sem.at[m, j], recv_sem=xr_sem.at[m, j],
            device_id={"col": 1 - col}, device_id_type=MESH,
        )

    def moments(m):
        return pltpu.make_async_remote_copy(
            src_ref=ssend.at[m], dst_ref=srecv.at[m],
            send_sem=ss_sem.at[m], recv_sem=sr_sem.at[m],
            device_id={"col": 1 - col}, device_id_type=MESH,
        )

    def partial(m, k):
        return pltpu.make_async_remote_copy(
            src_ref=psend.at[m, row_at(k)], dst_ref=precv.at[m, k],
            send_sem=ps_sem.at[m, k], recv_sem=pr_sem.at[m, k],
            device_id={"row": row_at(k)}, device_id_type=MESH,
        )

    partner = row + 1 - 2 * lax.rem(row, 2)
    across = 2 - row // 2
    beyond = 2 - 2 * (row // 2)
    hands_on = (row == 1) | (row == 2)
    targets = (row, partner, across)

    def first_feed(m, i):
        return pltpu.make_async_remote_copy(
            src_ref=feed.at[m, row], dst_ref=feed.at[m, row],
            send_sem=ns_sem.at[m, i], recv_sem=ar_sem.at[m, row],
            device_id={"row": targets[i]}, device_id_type=MESH,
        )

    def next_feed(m, i):
        return pltpu.make_async_remote_copy(
            src_ref=result.at[m], dst_ref=feed.at[m, row],
            send_sem=as_sem.at[m, i], recv_sem=ar_sem.at[m, row],
            device_id={"row": targets[i], "segment": 1}, device_id_type=MESH,
        )

    def passed(m, q, i):
        return pltpu.make_async_remote_copy(
            src_ref=feed.at[m, q], dst_ref=feed.at[m, q],
            send_sem=fs_sem.at[m, i], recv_sem=ar_sem.at[m, q],
            device_id={"row": partner}, device_id_type=MESH,
        )

    def mine_at(c):
        return pl.ds(pl.multiple_of(c * here, here), here)

    def latent(m, h, c):
        return pltpu.make_async_remote_copy(
            src_ref=lat_ref.at[m, :, pl.ds(h * part, part)],
            dst_ref=feed.at[m, work_row(h), mine_at(col)],
            send_sem=is_sem.at[m, h], recv_sem=ir_sem.at[m, c],
            device_id={"row": work_row(h), "col": work_col}, device_id_type=MESH,
        )

    def finished(m, c, h):
        at = pl.ds(pl.multiple_of(lax.rem(row, 2) * part, 128), part)
        return pltpu.make_async_remote_copy(
            src_ref=result.at[m, pl.ds(c * here, here)],
            dst_ref=landed.at[m, :, at],
            send_sem=os_sem.at[m, c], recv_sem=or_sem.at[m, h],
            device_id={"row": placed_row, "col": c}, device_id_type=MESH,
        )

    def last_bias():
        return pltpu.make_async_remote_copy(
            src_ref=bout_ref.at[:, pl.ds(pl.multiple_of(col * part, 128), part)], dst_ref=bout,
            send_sem=bs_sem.at[0], recv_sem=br_sem.at[0],
            device_id={"row": work_row(col), "col": work_col}, device_id_type=MESH,
        )

    def send_latents(m):
        for h in range(2):
            own = works_own(h)

            @pl.when(own)
            def _():
                feed[m, row, mine_at(col)] = lat_ref[m, :, h * part:(h + 1) * part]

            @pl.when(jnp.logical_not(own))
            def _():
                latent(m, h, col).start()

    def spread_latents(m):
        for c in range(COLS):
            @pl.when(jnp.logical_not((placed_row == row) & (col == c)))
            def _():
                latent(m, 0, c).wait_recv()
        for i in (2, 1):
            first_feed(m, i).start()

    def measure(m):
        for i in range(2):
            passed(m, beyond + i, i).wait_recv()

            @pl.when(hands_on)
            def _():
                passed(m, beyond + i, i).start()

        passed(m, partner, 0).wait_recv()

        @pl.when(seg == 1)
        def _():
            passed(m, row, 0).wait_recv()

        sums = jnp.zeros((feed.shape[2], 1), jnp.float32)
        for q in range(ROWS):
            sums += jnp.sum(feed[m, q].astype(jnp.float32), axis=-1, keepdims=True)
        mean = sums / half
        spread = jnp.zeros_like(sums)
        for q in range(ROWS):
            off = feed[m, q].astype(jnp.float32) - mean
            spread += jnp.sum(off * off, axis=-1, keepdims=True)
        lane = lax.broadcasted_iota(jnp.int32, ssend.shape[1:], 1)
        ssend[m] = jnp.where(lane == 0, mean, spread)
        moments(m).start()

    def enter(m):
        moments(m).wait_recv()
        mine, theirs = ssend[m], srecv[m]
        gap = mine[:, 0:1] - theirs[:, 0:1]
        mean = 0.5 * (mine[:, 0:1] + theirs[:, 0:1])
        var = (mine[:, 1:2] + theirs[:, 1:2] + (0.5 * half) * gap * gap) / (2 * half)
        inverse = lax.rsqrt(var + 1e-06)
        for q in range(ROWS):
            at = pl.ds(pl.multiple_of(col * half + q * part, 128), part)
            normed = (feed[m, q].astype(jnp.float32) - mean) * inverse
            ready[:, q * part:(q + 1) * part] = (
                normed * (1.0 + mods_ref[m, 1:2, at]) + mods_ref[m, 0:1, at]
            ).astype(jnp.bfloat16)

        @pl.when((m + 1 < micros) & ((seg == 1) | (m >= 1)))
        def _():
            measure(m + 1)

        @pl.loop(0, blocks)
        def _(j):
            at = pl.ds(pl.multiple_of(j * BLOCK, BLOCK), BLOCK)
            product = jnp.dot(ready[...], win[:, at], preferred_element_type=jnp.float32)
            xsend[m, j] = product.astype(jnp.bfloat16)
            exchange(m, j).start()
            pre[lax.rem(m, 2), j] = product + bin_ref[:, at]

        @pl.when(seg == 0)
        def _():
            @pl.when((m == 0) & (micros > 1))
            def _():
                measure(m + 1)

            @pl.when(m + 2 < micros)
            def _():
                spread_latents(m + 2)

    def middle(m):
        total[...] = jnp.zeros_like(total)

        @pl.loop(0, blocks)
        def _(j):
            exchange(m, j).wait_recv()
            at = pl.ds(pl.multiple_of(j * BLOCK, BLOCK), BLOCK)
            hidden = gelu(pre[lax.rem(m, 2), j] + xrecv[m, j].astype(jnp.float32))
            total[...] += jnp.dot(
                hidden.astype(jnp.bfloat16), wout[at, :], preferred_element_type=jnp.float32
            )

        for q in range(ROWS):
            psend[m, q] = total[:, q * part:(q + 1) * part].astype(jnp.bfloat16)
        for k in range(1, ROWS):
            partial(m, k).start()

    def leave(m):
        branch = psend[m, row].astype(jnp.float32)
        for k in range(1, ROWS):
            partial(m, k).wait_recv()
            branch += precv[m, k].astype(jnp.float32)
        at = pl.ds(pl.multiple_of(col * half + row * part, 128), part)
        act = feed[m, row].astype(jnp.float32) + mods_ref[m, 2:3, at] * (branch + bout[0:1, :])
        result[m] = act.astype(jnp.bfloat16)

        @pl.when(seg == 0)
        def _():
            for i in (2, 1, 0):
                next_feed(m, i).start()

        for c in range(COLS):
            own = (placed_row == row) & (col == c)

            @pl.when(jnp.logical_not(own))
            def _():
                finished(m, c, lax.rem(row, 2)).start()

            for h in range(2):
                @pl.when(own & (lax.rem(row, 2) == h))
                def _():
                    landed[m, :, h * part:(h + 1) * part] = result[m, c * here:(c + 1) * here]

    @pl.when(seg == 0)
    def _():
        @pl.loop(0, micros)
        def _(m):
            send_latents(m)

    own_bias = works_own(col)

    @pl.when(own_bias)
    def _():
        for h in range(2):
            @pl.when(col == h)
            def _():
                bout[...] = bout_ref[:, h * part:(h + 1) * part]

    @pl.when(jnp.logical_not(own_bias))
    def _():
        last_bias().start()

    @pl.when(seg == 0)
    def _():
        spread_latents(0)
        if micros > 1:
            spread_latents(1)

    measure(0)
    load_in.wait()

    @pl.loop(0, micros + 2)
    def _(i):
        @pl.when(i < micros)
        def _():
            enter(i)

        @pl.when(i == 1)
        def _():
            load_out.wait()

            @pl.when(jnp.logical_not((placed_row == row) & (lax.rem(row, 2) == col)))
            def _():
                last_bias().wait_recv()

        @pl.when(i >= 2)
        def _():
            leave(i - 2)

        @pl.when((i >= 1) & (i <= micros))
        def _():
            middle(i - 1)

    @pl.when(jnp.logical_not(own_bias))
    def _():
        last_bias().wait_send()

    @pl.loop(0, micros)
    def _(m):
        for h in range(2):
            @pl.when(jnp.logical_not(works_own(h)))
            def _():
                finished(m, 0, h).wait_recv()

        out_ref[m] = landed[m]
        moments(m).wait_send()
        for k in range(1, ROWS):
            partial(m, k).wait_send()

        @pl.loop(0, blocks)
        def _(j):
            exchange(m, j).wait_send()

        for c in range(COLS):
            @pl.when(jnp.logical_not((placed_row == row) & (col == c)))
            def _():
                finished(m, c, 0).wait_send()

        @pl.when(hands_on)
        def _():
            for i in range(2):
                passed(m, beyond + i, i).wait_send()

        @pl.when(seg == 0)
        def _():
            for i in range(3):
                next_feed(m, i).wait_send()
            for i in (1, 2):
                first_feed(m, i).wait_send()
            for h in range(2):
                @pl.when(jnp.logical_not(works_own(h)))
                def _():
                    latent(m, h, 0).wait_send()


def stationary(latents, w_in, b_in, w_out, b_out, modulation):
    micros, here, width = latents.shape
    tokens, part = COLS * here, width // 2
    half, units = w_in.shape[1:]
    blocks = units // BLOCK
    vmem = pl.BlockSpec(memory_space=pltpu.VMEM)
    hbm = pl.BlockSpec(memory_space=pl.ANY)
    bf16, f32, dma = jnp.bfloat16, jnp.float32, pltpu.SemaphoreType.DMA
    done = pl.pallas_call(
        functools.partial(kernel, micros, blocks),
        out_shape=jax.ShapeDtypeStruct(latents.shape, bf16),
        in_specs=[vmem, hbm, vmem, hbm, vmem, vmem],
        out_specs=vmem,
        scratch_shapes=[
            pltpu.VMEM((half, units), bf16),
            pltpu.VMEM((units, half), bf16),
            pltpu.VMEM((micros, ROWS, tokens, part), bf16),
            pltpu.VMEM((tokens, half), bf16),
            pltpu.VMEM((2, blocks, tokens, BLOCK), f32),
            pltpu.VMEM((micros, blocks, tokens, BLOCK), bf16),
            pltpu.VMEM((micros, blocks, tokens, BLOCK), bf16),
            pltpu.VMEM((tokens, half), f32),
            pltpu.VMEM((micros, ROWS, tokens, part), bf16),
            pltpu.VMEM((micros, ROWS, tokens, part), bf16),
            pltpu.VMEM((micros, tokens, 128), f32),
            pltpu.VMEM((micros, tokens, 128), f32),
            pltpu.VMEM((micros, tokens, part), bf16),
            pltpu.VMEM((micros, here, width), bf16),
            pltpu.VMEM((8, part), f32),
            dma((2,)),
            dma((micros, blocks)),
            dma((micros, blocks)),
            dma((micros,)),
            dma((micros,)),
            dma((micros, ROWS)),
            dma((micros, ROWS)),
            dma((micros, ROWS)),
            dma((micros, ROWS)),
            dma((micros, 2)),
            dma((micros, COLS)),
            dma((micros, COLS)),
            dma((micros, 2)),
            dma((1,)),
            dma((1,)),
            dma((micros, 2)),
            dma((micros, ROWS)),
        ],
        compiler_params=pltpu.CompilerParams(
            collective_id=0, has_side_effects=True, vmem_limit_bytes=62 * 1024 * 1024
        ),
        cost_estimate=pl.CostEstimate(
            flops=4 * micros * tokens * half * units,
            bytes_accessed=4 * half * units,
            transcendentals=micros * tokens * units,
        ),
    )(latents, w_in[0], b_in, w_out[0], jnp.broadcast_to(b_out, (8, width)), modulation[0])
    return done[None]


def solution(mesh):
    sizes = dict(mesh.shape)
    fits = (sizes["row"], sizes["col"], sizes["segment"]) == (ROWS, COLS, SEGS)

    def on_device(latents, w_in, *rest):
        aligned = latents.shape[2] % 256 == 0 and w_in.shape[2] % BLOCK == 0
        chosen = stationary if fits and aligned else general
        return chosen(latents, w_in, *rest)

    return jax.shard_map(
        on_device,
        mesh=mesh,
        in_specs=(
            P(None, ("groups", "col"), "row"),
            P("segment", "col", "row"),
            P("segment", "row"),
            P("segment", "row", "col"),
            P("segment", "row"),
            P("segment", "groups", None, None),
        ),
        out_specs=P("segment", None, ("groups", "col"), "row"),
        check_vma=False,
    )
```
